128 devices in a mesh: section: 8 (over z, core), expert: 16 (over y, x).
Axes of the slice: x: 4, y: 4, z: 4, core: 2. Of those that a mesh axis runs over, the one named last changes fastest.
Arguments:
- d_output: bfloat16 [16384, 4096], P(('section', 'expert')), may hold values from -3 to 3
- gate_values: bfloat16 [16384, 8], P(('section', 'expert')), may hold values from 0.049804688 to 0.5
- routes: int32 [16384, 8], P(('section', 'expert')), may hold values from 0 to 31, all different within a row; in each aligned block of 128 rows (0 to 127, 128 to 255, ...) at most 40 rows name the same one
- hidden_saved: bfloat16 [8, 32, 16, 40, 768], P('section', 'expert'), may hold values from -3 to 3
- w_down: bfloat16 [32, 768, 4096], P('expert'), may hold values from -0.21875 to 0.21875
Outputs:
- d_hidden: bfloat16 [8, 32, 16, 40, 768], P('section', 'expert')
- d_weight: bfloat16 [32, 768, 4096], P('expert', 'section')
- d_gate: float32 [16384, 8], P(('section', 'expert'))
The draws below stay inside these ranges and needn't reach their ends.
Inputs may be any that keep to these rules, and one draw needn't show every extreme that they name: `routes`: each row names 8 different experts. Within the rows of one device (128 tokens) no expert is named by more than 40 rows, a bound that some block reaches.
All inputs are finite; a program needn't handle non-finite values.
Results may differ from the reference program's by a relative error of at most 0.017.
Values may be sent and summed in bfloat16 or wider, within the bound.
No kernel may reach another device: no remote copies, remote signals or barrier semaphores. Data moves between devices by JAX's collectives and lax.ppermute only.
A program may use at most 192 MiB of HBM per device.

```python
import math
import jax
import jax.numpy as jnp
import numpy as np
from jax import lax

D = 4096
FF = 768
TOPK = 8
TOK_DEV = 128
EXPERTS = 32
CAP = 40
SLICES = 8
TOKENS = 16384
N_EXPERT = 16


def block_levels(key, shape, pieces, least, largest):
    factor_of, own = 1.0, jax.random.fold_in(key, 6)
    for axis_at, blocks in pieces:
        heights = jnp.exp(jax.random.uniform(jax.random.fold_in(own, axis_at), (blocks,), jnp.float32, least / len(pieces), largest / len(pieces)))
        factor_of = factor_of * jnp.repeat(heights, shape[axis_at] // blocks).reshape([-1 if axis == axis_at else 1 for axis in range(len(shape))])
    return factor_of


def assign_block(own_key, own, number, rows, amount, top, limit, skew):
    order = jax.random.permutation(own_key, amount)
    heavy_load, ordinary = portions_of(amount, rows * top, limit, skew, True), portions_of(amount, rows * top, limit, skew, False)
    places = jnp.arange(amount)

    def named(tallies, offset_by):
        used = int((tallies > 0).sum())
        fixed = max(1, used // 4)
        shifted = fixed + (places - fixed + offset_by * (used - fixed)) % max(1, amount - fixed)
        return jnp.zeros((amount,), jnp.int32).at[order[jnp.where(places < fixed, places, shifted)]].set(jnp.asarray(tallies, jnp.int32))

    tallies = jnp.where(number % 4 == 0, named(heavy_load, number // 4), named(ordinary, number - number // 4 - 1))
    mixed = jax.random.permutation(jax.random.fold_in(own, 3), amount)
    donor, taker = mixed[0:amount // 2 * 2:2], mixed[1:amount // 2 * 2:2]
    margin = jnp.minimum(tallies[donor] - 1, limit - tallies[taker]) // 2
    margin = jnp.where((donor == order[0]) | (taker == order[0]) | (tallies[taker] == 0), 0, jnp.maximum(margin, 0))
    shifted = jax.random.randint(jax.random.fold_in(own, 4), (amount // 2,), 0, 1 << 20) % (margin + 1)
    tallies = tallies.at[donor].add(-shifted).at[taker].add(shifted)
    labels = jnp.searchsorted(jnp.cumsum(tallies), jnp.arange(rows * top), side="right").astype(jnp.int32)
    listing = labels.reshape(top, rows).T
    listing = listing[jax.random.permutation(jax.random.fold_in(own, 1), rows)]
    offset_by = jax.random.randint(jax.random.fold_in(own, 2), (rows, 1), 0, top)
    return jnp.take_along_axis(listing, (jnp.arange(top)[None, :] + offset_by) % top, axis=1)


def portions_of(count, total, bound, lean, full):
    portions = [(1 << 20) // math.isqrt(grade ** lean) + 1 for grade in range(1, count + 1)]
    largest = bound if full else min(bound, max(-(-total // count), total * portions[0] // sum(portions)))
    least = 1 if total - largest >= count - 1 else 0
    given, rest = [largest] + [least] * (count - 1), total - largest - least * (count - 1)
    while rest > 0:
        candidates = [i for i in range(1, count) if given[i] < largest] or [i for i in range(1, count) if given[i] < bound]
        pool, budget = sum([portions[i] for i in candidates]), rest
        for i in candidates:
            addition = min(bound - given[i], max(1, budget * portions[i] // pool), rest)
            given[i] = given[i] + addition
            rest = rest - addition
    return np.array(given)


def normal_values(stream_key, shape, spread, most, cuts=(), held_as=jnp.bfloat16):
    gain = block_levels(stream_key, shape, cuts, -0.22, 0.18) if cuts else 1.0
    drawn = jax.random.normal(stream_key, shape, jnp.float32) * spread * gain
    return jnp.minimum(jnp.maximum(drawn, -most), most).astype(held_as)


def setup_inputs(seed: int = 0) -> dict:
    splits = jax.random.split(jax.random.key(seed), 6)
    d_output = normal_values(splits[0], (TOKENS, D), 0.5, 3.0, ((0, 128),))
    gate_values = jnp.clip(jnp.exp(math.log(0.5) - 2.306499 * jax.random.uniform(splits[1], (TOKENS, TOPK), jnp.float32) ** block_levels(splits[1], (TOKENS, TOPK), ((0, 128),), -0.2, 0.2)), 0.049804688, 0.5).astype(jnp.bfloat16)
    routes_keys = jax.random.split(jax.random.fold_in(splits[2], 1), TOKENS // TOK_DEV)
    routes_turns = jax.random.permutation(jax.random.fold_in(splits[2], 3), TOKENS // TOK_DEV)
    routes = jax.vmap(lambda own, number: assign_block(jax.random.fold_in(splits[2], 2), own, number, TOK_DEV, EXPERTS, TOPK, CAP, 2))(routes_keys, routes_turns).reshape((TOKENS, TOPK))
    hidden_saved = normal_values(splits[3], (SLICES, EXPERTS, N_EXPERT, CAP, FF), 0.5, 3.0, ((0, 8), (1, 16)))
    w_down = normal_values(splits[4], (EXPERTS, FF, D), FF ** -0.5, 0.21875, ((0, 16),))
    return {"d_output": d_output, "gate_values": gate_values, "routes": routes, "hidden_saved": hidden_saved, "w_down": w_down}


def slot_ranks(route_block, expert_count):
    one_hot = (route_block[..., None] == jnp.arange(expert_count, dtype=jnp.int32)).astype(jnp.int32)
    earlier = jnp.cumsum(one_hot, axis=1) - one_hot
    return jnp.sum(earlier * one_hot, axis=2)


def reference(d_output, gate_values, routes, hidden_saved, w_down):
    weight_wide = w_down.astype(jnp.float32)
    pair_count = TOK_DEV * TOPK
    dy_all = d_output.reshape(SLICES, N_EXPERT * TOK_DEV, D)
    gate_all = gate_values.reshape(SLICES, N_EXPERT * TOK_DEV, TOPK)
    route_all = routes.reshape(SLICES, N_EXPERT * TOK_DEV, TOPK)

    def per_slice(weight_total, inputs):
        dy_slice, gate_slice, route_slice, hidden_slice = inputs
        route_block = route_slice.reshape(N_EXPERT, pair_count).astype(jnp.int32)
        slot_rank = slot_ranks(route_block, EXPERTS)
        source_dev = jnp.arange(N_EXPERT, dtype=jnp.int32)[:, None]
        slot_index = (route_block * (N_EXPERT * CAP) + source_dev * CAP + slot_rank).reshape(-1).astype(jnp.int32)
        gated = (gate_slice.astype(jnp.float32)[:, :, None] * dy_slice.astype(jnp.float32)[:, None, :]).astype(jnp.bfloat16)
        dispatched = jnp.zeros((EXPERTS * N_EXPERT * CAP, D), jnp.bfloat16).at[slot_index].set(gated.reshape(-1, D))
        dispatched = dispatched.reshape(EXPERTS, N_EXPERT * CAP, D).astype(jnp.float32)
        hidden_wide = hidden_slice.reshape(EXPERTS, N_EXPERT * CAP, FF).astype(jnp.float32)
        d_hidden_slice = jnp.einsum("erd,efd->erf", dispatched, weight_wide).astype(jnp.bfloat16)
        partial_value = jnp.einsum("erf,erd->efd", hidden_wide, dispatched).astype(jnp.bfloat16)
        partial_value = lax.optimization_barrier(partial_value).astype(jnp.float32)
        expert_rows = jnp.einsum("erf,efd->erd", hidden_wide, weight_wide).astype(jnp.bfloat16)
        picked = expert_rows.reshape(-1, D)[slot_index].reshape(N_EXPERT * TOK_DEV, TOPK, D)
        d_gate_slice = jnp.sum(dy_slice.astype(jnp.float32)[:, None, :] * picked.astype(jnp.float32), axis=2)
        return weight_total + partial_value, (d_hidden_slice.reshape(EXPERTS, N_EXPERT, CAP, FF), d_gate_slice)

    start = jnp.zeros((EXPERTS, FF, D), jnp.float32)
    weight_total, (d_hidden, d_gate) = lax.scan(per_slice, start, (dy_all, gate_all, route_all, hidden_saved))
    return d_hidden, weight_total.astype(jnp.bfloat16), d_gate.reshape(TOKENS, TOPK)
```

```python
import jax
import jax.numpy as jnp
from jax import lax
from jax.experimental import pallas as pl
from jax.experimental.pallas import tpu as pltpu
from jax.sharding import PartitionSpec as P

AXES = ("section", "expert")
CHUNKS = (1024, 1024, 1024, 1024)
TILE = 512
DEEP = 1024
VMEM_LIMIT = 20 * 1024 * 1024
COSTS = {"o": 20, "a": 20, "r": 20, "I": 20, "P": 20, "T": 20, "p": 20, "w": 20, "m": 20, "s": 20, "t": 20, "e": 20, "h": 20, "H": 20}
PLAN = (
    "a0", "a1", "I", "o2", "o3", "r0", "r1", "a2", "a3", "P", "T", "r2", "r3", "p0", "p1", "p2",
    "p3", "w0", "m0", "w1", "m1", "s0", "s1", "h", "w2", "w3", "t0", "t1", "m2", "m3", "s2",
    "s3", "H", "t2", "t3", "e",
)
F32, BF16 = jnp.float32, jnp.bfloat16


def moves(move):
    pairs = []
    for z in range(4):
        for core in range(2):
            for y in range(4):
                for x in range(4):
                    tz, tcore, ty, tx = move(z, core, y, x)
                    pairs.append(
                        (
                            ((z * 2 + core) * 4 + y) * 4 + x,
                            ((tz % 4 * 2 + tcore) * 4 + ty % 4) * 4 + tx % 4,
                        )
                    )
    return pairs


MEET = ((1, 3), (3, 1))


def along(axis, step, parity=0):
    def move(z, core, y, x):
        mask = MEET[core][(step + parity) % 2]
        if axis == "z":
            return (z ^ mask, core, y, x)
        if (axis == "first") == (core == 0):
            return (z, core, y, x ^ mask)
        return (z, core, y ^ mask, x)

    return moves(move)


SWAP = moves(lambda z, core, y, x: (z, 1 - core, y, x))


def send(value, pairs):
    return lax.ppermute(value, AXES, pairs)


class Order:
    def __init__(self):
        self.token = None
        self.cost = 0


ORDER = Order()


def call(kernel, grid, inputs, outputs, scratch=()):
    held = [] if ORDER.token is None else [ORDER.token]
    unused = len(held)

    def run(*refs):
        body = list(refs[unused:])
        body.pop(len(inputs) + len(outputs))[...] = jnp.zeros((8, 128), F32)
        kernel(*body)

    *results, ORDER.token = pl.pallas_call(
        run,
        grid=grid,
        in_specs=[pl.BlockSpec(memory_space=pltpu.HBM)] * unused + [spec for _, spec in inputs],
        out_specs=[spec for _, spec in outputs] + [whole((8, 128))],
        out_shape=[shape for shape, _ in outputs] + [out(8, 128, dtype=F32)],
        scratch_shapes=list(scratch),
        compiler_params=pltpu.CompilerParams(vmem_limit_bytes=VMEM_LIMIT),
        cost_estimate=pl.CostEstimate(
            flops=int(ORDER.cost * 10**9), bytes_accessed=0, transcendentals=0
        ),
    )(*held, *[value for value, _ in inputs])
    return results


def whole(shape):
    return pl.BlockSpec(shape, lambda *_: (0,) * len(shape))


def columns(shape, offset=0):
    lead = (0,) * (len(shape) - 1)
    return pl.BlockSpec(tuple(shape[:-1]) + (TILE,), lambda i: lead + (i + offset // TILE,))


def out(*shape, dtype=BF16):
    return jax.ShapeDtypeStruct(shape, dtype)


SMEM = pl.BlockSpec(memory_space=pltpu.SMEM)


def mm(a, b):
    return jnp.dot(a, b, preferred_element_type=F32)


def mm_turned(a, b):
    return lax.dot_general(a, b, (((1,), (1,)), ((), ())), preferred_element_type=F32)


PIECES = ((0, 0), (0, 1), (0, 2), (2, 0), (2, 1), (1, 0), (1, 2))
RANKED = [(0, r) for r in range(16)] + [
    (g, r) for g in (1, 2) for line in (0, 3 - g) for r in range(line * 4, line * 4 + 4)
]


def prepare(at, info, cap, held):
    sources, _, tokens = info.shape
    row_of = {(g, r, e): n * held + e for n, (g, r) in enumerate(RANKED) for e in range(held)}
    rows = len(row_of)
    packed, line = held * 4 * cap, 4 * tokens

    def kernel(at_ref, info_ref, pick_ref, key_ref, gate_ref, named_ref):
        for n, (g, r) in enumerate(RANKED):
            block = info_ref[at_ref[r]].astype(F32)
            for e in range(held):
                expert = at_ref[16 + g * held + e].astype(F32)
                hit = block[:8] == expert
                named_ref[n * held + e : n * held + e + 1, :] = jnp.max(
                    jnp.where(hit, 1.0, 0.0), axis=0, keepdims=True
                )
                if g == 0:
                    gate_ref[n * held + e : n * held + e + 1, :] = jnp.sum(
                        jnp.where(hit, block[8:], 0.0), axis=0, keepdims=True
                    )
        named = named_ref[...]
        first = lax.broadcasted_iota(jnp.int32, (tokens, tokens), 0)
        second = lax.broadcasted_iota(jnp.int32, (tokens, tokens), 1)
        before = jnp.where(first < second, 1.0, 0.0).astype(BF16)
        key = jnp.where(named > 0.5, mm(named.astype(BF16), before), -1.0)
        key_ref[...] = key[: sources * held]
        named_ref[...] = key
        slot = lax.broadcasted_iota(jnp.int32, (cap, tokens), 0).astype(F32)
        none = jnp.zeros((cap, tokens), F32)
        for n, (g, l) in enumerate(PIECES):
            for s in range(4):
                parts = []
                for e in range(held):
                    row = row_of[g, l * 4 + s, e]
                    mine = jnp.where(slot == named_ref[row : row + 1, :], 1.0, 0.0)
                    parts += [mine if t == s else none for t in range(4)]
                pick_ref[n, :, s * tokens : (s + 1) * tokens] = jnp.concatenate(parts, axis=0).astype(BF16)

    return call(
        kernel,
        (1,),
        [(at, SMEM), (info, whole(info.shape))],
        [
            (out(len(PIECES), packed, line), whole((len(PIECES), packed, line))),
            (out(sources * held, tokens, dtype=F32), whole((sources * held, tokens))),
            (out(sources * held, tokens, dtype=F32), whole((sources * held, tokens))),
        ],
        scratch=[pltpu.VMEM((rows, tokens), F32)],
    )


def slot_hits(key_ref, row, cap):
    key = key_ref[row : row + 1, :]
    slot = lax.broadcasted_iota(jnp.int32, (cap, key.shape[1]), 0).astype(F32)
    return slot == key


def turn_hidden(at, key, gate, hidden):
    held, sources, cap, ff = hidden.shape
    block = ff // 8

    def kernel(at_ref, key_ref, gate_ref, hidden_ref, out_ref):
        for e in range(held):
            parts = []
            for r in range(sources):
                row = r * held + e
                weight = jnp.sum(
                    jnp.where(slot_hits(key_ref, row, cap), gate_ref[row : row + 1, :], 0.0),
                    axis=1,
                    keepdims=True,
                )
                parts.append(hidden_ref[e, at_ref[r]].astype(F32) * weight)
            turned = jnp.concatenate(parts, axis=0).T.astype(BF16)
            for b in range(8):
                out_ref[at_ref[24 + b], e] = turned[b * block : (b + 1) * block]

    shape = (8, held, block, sources * cap)
    return call(
        kernel,
        (1,),
        [(at, SMEM), (key, whole(key.shape)), (gate, whole(gate.shape)), (hidden, whole(hidden.shape))],
        [(out(*shape), whole(shape))],
    )[0]


def share(info, sources):
    def kernel(info_ref, out_ref):
        out_ref[...] = jnp.broadcast_to(info_ref[...].astype(BF16)[None], out_ref.shape)

    shape = (sources,) + info.shape
    return call(kernel, (1,), [(info, whole(info.shape))], [(out(*shape), whole(shape))])[0]


def own_rows(d_output, offset, size):
    tokens = d_output.shape[0]

    def kernel(in_ref, out_ref):
        out_ref[...] = in_ref[...]

    return call(
        kernel,
        (size // TILE,),
        [(d_output, columns(d_output.shape, offset))],
        [(out(tokens, size), columns((tokens, size)))],
    )[0]


def join(d_output, offset, pieces):
    tokens, size = d_output.shape[0], pieces[0][0].shape[1]

    def spec(at):
        return pl.BlockSpec((tokens, TILE), lambda i: (at, i))

    def kernel(*refs):
        for n, ref in enumerate(refs[:-1]):
            refs[-1][n * tokens : (n + 1) * tokens, :] = ref[...]

    shape = (tokens * (1 + len(pieces)), size)
    return call(
        kernel,
        (size // TILE,),
        [(d_output, columns(d_output.shape, offset))] + [(b, spec(at)) for b, at in pieces],
        [(out(*shape), columns(shape))],
    )[0]


def pack(rows, far, pick, held, parity):
    line, size = rows.shape
    count = pick.shape[1]
    per = count // held
    shape = (held, 2 * per, size)
    near, there = 1 + parity, 2 - parity

    places = [(group, start) for group in (there, 0) for start in (0, near)]

    def kernel(rows_ref, far_ref, *refs):
        picks, (here_ref, there_ref) = refs[:4], refs[4:]
        for k, pick_ref in enumerate(picks):
            chosen = mm(pick_ref[0], (rows_ref, far_ref)[k % 2][...]).astype(BF16)
            target, n = (there_ref, here_ref)[k // 2], k % 2
            for e in range(held):
                target[e, n * per : (n + 1) * per, :] = chosen[e * per : (e + 1) * per]

    def piece(place):
        at = PIECES.index(place)
        return pl.BlockSpec((1, count, line), lambda i: (at, 0, 0))

    return call(
        kernel,
        (size // TILE,),
        [(rows, columns(rows.shape)), (far, columns(far.shape))]
        + [(pick, piece(place)) for place in places],
        [(out(*shape), columns(shape)), (out(*shape), columns(shape))],
    )


def collect(here, came, turned, parity):
    held, half, size = here.shape
    block, total = turned.shape[2:]
    per = half // 2
    places = ((0, 1), (2, 3)) if parity == 0 else ((0, 2), (1, 3))

    def kernel(here_ref, came_ref, turned_ref, slots_ref, other_ref):
        for e in range(held):
            for ref, lines in zip((here_ref, came_ref), places):
                for n, at in enumerate(lines):
                    slots_ref[e, at * per : (at + 1) * per, :] = ref[e, n * per : (n + 1) * per]
            left = turned_ref[:, e].reshape(4 * block, total)
            product = mm(left, slots_ref[e])
            for n in range(4):
                other_ref[n, e] = product[n * block : (n + 1) * block].astype(BF16)

    return call(
        kernel,
        (size // TILE,),
        [
            (here, columns(here.shape)),
            (came, columns(came.shape)),
            (turned, pl.BlockSpec((4, held, block, total), lambda i: (1, 0, 0, 0))),
        ],
        [
            (out(held, total, size), columns((held, total, size))),
            (out(4, held, block, size), columns((4, held, block, size))),
        ],
    )


def own_product(slots, turned):
    held, total, size = slots.shape
    block = turned.shape[2]

    def kernel(slots_ref, turned_ref, mine_ref):
        for e in range(held):
            product = mm(turned_ref[:, e].reshape(4 * block, total), slots_ref[e])
            for n in range(4):
                mine_ref[n, e] = product[n * block : (n + 1) * block].astype(BF16)

    return call(
        kernel,
        (size // TILE,),
        [
            (slots, columns(slots.shape)),
            (turned, pl.BlockSpec((4, held, block, total), lambda i: (0, 0, 0, 0))),
        ],
        [(out(4, held, block, size), columns((4, held, block, size)))],
    )[0]


def add_parts(terms):
    shape = (len(terms),) + terms[0][0][0].shape[1:]
    flat = [term for group in terms for term in group]
    width = len(terms[0])

    def spec(at):
        return pl.BlockSpec((1,) + shape[1:-1] + (TILE,), lambda i: (at, 0, 0, i))

    def kernel(*refs):
        for n in range(len(terms)):
            value = 0.0
            for ref in refs[n * width : (n + 1) * width]:
                value = value + ref[0].astype(F32)
            refs[-1][n] = value.astype(BF16)

    return call(
        kernel,
        (shape[-1] // TILE,),
        [(array, spec(at)) for array, at in flat],
        [(out(*shape), columns(shape))],
    )[0]


def finish(parts, width):
    _, held, block, _ = parts[0][0].shape
    counts = [group[0].shape[3] // TILE for group in parts]
    starts = [sum(counts[:n]) for n in range(len(counts))]
    terms = len(parts[0])

    def kernel(*refs):
        step = pl.program_id(0)
        for n, (start, count) in enumerate(zip(starts, counts)):

            @pl.when((step >= start) & (step < start + count))
            def _(n=n):
                value = 0.0
                for ref in refs[n * terms : (n + 1) * terms]:
                    value = value + ref[0].astype(F32)
                refs[-1][...] = value.astype(BF16)

    def spec(start, count):
        return pl.BlockSpec(
            (1, held, block, TILE),
            lambda i: (0, 0, 0, jnp.minimum(jnp.maximum(i - start, 0), count - 1)),
        )

    shape = (held, block, width)
    return call(
        kernel,
        (width // TILE,),
        [(part, spec(a, c)) for group, a, c in zip(parts, starts, counts) for part in group],
        [(out(*shape), columns(shape))],
    )[0]


def chunk_specs(halves, ff):
    rows = halves[0].shape[1]
    counts = [h.shape[2] // DEEP for h in halves]
    starts = [sum(counts[:n]) for n in range(len(halves))]

    def spec(start, count):
        return pl.BlockSpec(
            (1, rows, DEEP), lambda e, i: (e, 0, jnp.minimum(jnp.maximum(i - start, 0), count - 1))
        )

    specs = [spec(a, b) for a, b in zip(starts, counts)]
    return counts, starts, specs, pl.BlockSpec((1, ff, DEEP), lambda e, i: (e, 0, i))


def add_chunks(refs, starts, counts, lines, w_ref, sum_ref):
    step = pl.program_id(1)
    for n, (ref, start, count) in enumerate(zip(refs, starts, counts)):

        @pl.when((step >= start) & (step < start + count))
        def _(n=n, ref=ref):
            product = mm_turned(ref[0], w_ref[0])
            per = product.shape[0] // 2
            for k, line in enumerate(lines[n % 2]):
                sum_ref[line * per : (line + 1) * per, :] += product[k * per : (k + 1) * per]


HERE = ((0, 1), (0, 2))
CAME = ((2, 3), (1, 3))


def hidden_sums(halves, w_down):
    held, rows, _ = halves[0].shape
    ff, total = w_down.shape[1], 2 * rows
    counts, starts, specs, w_spec = chunk_specs(halves, ff)

    def kernel(*refs):
        w_ref, sum_ref, acc_ref = refs[len(halves) :]

        @pl.when(pl.program_id(1) == 0)
        def _():
            acc_ref[...] = jnp.zeros_like(acc_ref)

        add_chunks(refs, starts, counts, HERE, w_ref, acc_ref)

        @pl.when(pl.program_id(1) == sum(counts) - 1)
        def _():
            sum_ref[0] = acc_ref[...]

    return call(
        kernel,
        (held, sum(counts)),
        list(zip(halves, specs)) + [(w_down, w_spec)],
        [(out(held, total, ff, dtype=F32), pl.BlockSpec((1, total, ff), lambda e, i: (e, 0, 0)))],
        scratch=[pltpu.VMEM((total, ff), F32)],
    )[0]


def hidden_end(at, key, gate, hidden, sums, halves, w_down):
    held, sources, cap, ff = hidden.shape
    total = sums.shape[1]
    tokens = key.shape[1]
    counts, starts, specs, w_spec = chunk_specs(halves, ff)

    def kernel(at_ref, key_ref, gate_ref, hidden_ref, sums_ref, *refs):
        w_ref, d_hidden_ref, grad_ref, acc_ref = refs[len(halves) :]

        @pl.when(pl.program_id(1) == 0)
        def _():
            acc_ref[...] = sums_ref[0]

        add_chunks(refs, starts, counts, CAME, w_ref, acc_ref)

        def end(e):
            for r in range(sources):
                row = r * held + e
                hits = slot_hits(key_ref, row, cap)
                weight = jnp.sum(
                    jnp.where(hits, gate_ref[row : row + 1, :], 0.0), axis=1, keepdims=True
                )
                value = acc_ref[r * cap : (r + 1) * cap, :]
                place = at_ref[r]
                d_hidden_ref[0, place] = (value * weight).astype(BF16)
                dots = jnp.sum(value * hidden_ref[0, place].astype(F32), axis=1, keepdims=True)
                grad_ref[place, e : e + 1, :] = jnp.sum(
                    jnp.where(hits, dots, 0.0), axis=0, keepdims=True
                )

        for e in range(held):

            @pl.when((pl.program_id(1) == sum(counts) - 1) & (pl.program_id(0) == e))
            def _(e=e):
                end(e)

    by_expert = pl.BlockSpec((1, sources, cap, ff), lambda e, i: (e, 0, 0, 0))
    return call(
        kernel,
        (held, sum(counts)),
        [
            (at, SMEM),
            (key, whole(key.shape)),
            (gate, whole(gate.shape)),
            (hidden, by_expert),
            (sums, pl.BlockSpec((1, total, ff), lambda e, i: (e, 0, 0))),
        ]
        + list(zip(halves, specs))
        + [(w_down, w_spec)],
        [
            (out(*hidden.shape), by_expert),
            (out(sources, held, tokens, dtype=F32), whole((sources, held, tokens))),
        ],
        scratch=[pltpu.VMEM((total, ff), F32)],
    )


def shards(d_output, gate_values, routes, hidden_saved, w_down):
    ORDER.token = None
    tokens, width = d_output.shape
    hidden = hidden_saved[0]
    held, sources, cap, ff = hidden.shape

    section, group = lax.axis_index("section"), lax.axis_index("expert")
    z, core, y, x = section // 2, section % 2, group // 4, group % 4
    masks = jnp.stack([0 * core, 1 + 2 * core, 3 - 2 * core, 0 * core + 2])
    first_at = jnp.where(core == 0, x, y) ^ masks
    second_at = jnp.where(core == 0, y, x) ^ masks
    up_first, up_second = jnp.where(core == 0, 1, 4), jnp.where(core == 0, 4, 1)
    source_at = (second_at[:, None] * up_second + first_at[None, :] * up_first).reshape(-1)
    group_at = second_at[:4] * up_second + first_at[0] * up_first
    experts = (group_at[:, None] * held + jnp.arange(held)[None, :]).reshape(-1)
    section_at = jnp.arange(8)
    met = (section_at // 2) ^ z
    place = jnp.where(met == 2, 3, jnp.where(met == 0, 0, jnp.where((met == 1) == (section_at % 2 == 0), 2, 1)))
    is_mine = section_at % 2 == core
    at = jnp.concatenate([source_at, experts, jnp.where(is_mine, place, 4 + place)]).astype(jnp.int32)

    offsets = [sum(CHUNKS[:n]) for n in range(len(CHUNKS))]
    info = jnp.concatenate([routes.astype(F32), gate_values.astype(F32)], axis=1).T
    count = len(CHUNKS)
    one, two, rows, far, here, came, slots = ([None] * count for _ in range(7))
    got, mine, passed, more = ([None] * count for _ in range(4))
    for n in range(2):
        own = d_output[:, offsets[n] : offsets[n] + CHUNKS[n]]
        one[n] = send(own, along("first", 0, n % 2))

    for step in PLAN:
        kind, n = step[0], int(step[1:] or 0)
        parity = n % 2
        ORDER.cost = COSTS[kind]
        if kind == "o":
            one[n] = send(own_rows(d_output, offsets[n], CHUNKS[n]), along("first", 0, parity))
        elif kind == "I":
            all_info = lax.all_to_all(share(info, sources), "expert", 0, 0, tiled=True)
        elif kind == "P":
            pick, key, gate = prepare(at, all_info, cap, held)
        elif kind == "T":
            turned = turn_hidden(at, key, gate, hidden)
        elif kind == "a":
            two[n] = send(join(d_output, offsets[n], [(one[n], 0)]), along("first", 1, parity))
        elif kind == "r":
            came_rows = [(one[n], 0), (two[n], 0), (two[n], 1)]
            if parity == 1:
                came_rows = [(two[n], 0), (one[n], 0), (two[n], 1)]
            rows[n] = join(d_output, offsets[n], came_rows)
            far[n] = send(rows[n], along("second", 0, parity))
        elif kind == "p":
            here[n], there = pack(rows[n], far[n], pick, held, parity)
            came[n] = send(there, along("second", 1, parity))
        elif kind == "w":
            slots[n], other = collect(here[n], came[n], turned, parity)
            got[n] = send(other, SWAP)
        elif kind == "m":
            mine[n] = own_product(slots[n], turned)
        elif kind == "s":
            sums = add_parts([[(mine[n], k), (got[n], k)] for k in (2 - parity, 3)])
            passed[n] = send(sums, along("z", 0, parity))
        elif kind == "t":
            sums = add_parts([[(mine[n], 1 + parity), (got[n], 1 + parity), (passed[n], 1)]])
            more[n] = send(sums, along("z", 1, parity))
        elif kind == "e":
            parts = [(mine[k], got[k], passed[k], more[k]) for k in range(count)]
            d_weight = finish(parts, width)
        elif kind == "h":
            hidden_part = hidden_sums(here, w_down)
        elif kind == "H":
            d_hidden, token_grad = hidden_end(at, key, gate, hidden, hidden_part, came, w_down)
    returned = lax.all_to_all(token_grad, "expert", 0, 0, tiled=True).reshape(-1, tokens)
    chosen = routes.T[None] == jnp.arange(sources * held)[:, None, None]
    d_gate = jnp.sum(jnp.where(chosen, returned[:, None, :], 0.0), axis=0).T
    return (d_hidden[None], d_weight, d_gate)


def solution(mesh):
    placed = (
        P(("section", "expert"), None),
        P(("section", "expert"), None),
        P(("section", "expert"), None),
        P("section", "expert", None, None, None),
        P("expert", None, None),
    )
    return jax.shard_map(
        shards,
        mesh=mesh,
        in_specs=placed,
        out_specs=(
            P("section", "expert", None, None, None),
            P("expert", "section", None),
            P(("section", "expert"), None),
        ),
        check_vma=False,
    )
```

```python
import jax
import jax.numpy as jnp
from jax import lax
from jax.experimental import pallas as pl
from jax.experimental.pallas import tpu as pltpu
from jax.sharding import PartitionSpec as P

AXES = ("section", "expert")
CHUNKS = (1024, 1024, 1024, 1024)
TILE = 512
DEEP = 1024
VMEM_LIMIT = 20 * 1024 * 1024
PLAN = (
    "a0", "a1", "o2", "o3-", "r0-", "r1", "a2", "a3", "I-", "P-", "T-", "r2", "r3", "p0", "p1",
    "h0", "p2", "p3", "h1", "w0", "m0", "w1", "m1", "s0", "s1", "w2", "w3", "m2", "m3", "s2",
    "s3", "H", "t0-", "t1-", "t2-", "t3-", "e",
)
F32, BF16 = jnp.float32, jnp.bfloat16


def moves(move):
    pairs = []
    for z in range(4):
        for core in range(2):
            for y in range(4):
                for x in range(4):
                    tz, tcore, ty, tx = move(z, core, y, x)
                    pairs.append(
                        (
                            ((z * 2 + core) * 4 + y) * 4 + x,
                            ((tz % 4 * 2 + tcore) * 4 + ty % 4) * 4 + tx % 4,
                        )
                    )
    return pairs


MEET = ((1, 3), (3, 1))


def along(axis, step, parity=0):
    def move(z, core, y, x):
        mask = MEET[core][(step + parity) % 2]
        if axis == "z":
            return (z ^ mask, core, y, x)
        if (axis == "first") == (core == 0):
            return (z, core, y, x ^ mask)
        return (z, core, y ^ mask, x)

    return moves(move)


SWAP = moves(lambda z, core, y, x: (z, 1 - core, y, x))


def send(value, pairs):
    return lax.ppermute(value, AXES, pairs)


class Order:
    def __init__(self):
        self.token = None
        self.cost = 0


ORDER = Order()


def call(kernel, grid, inputs, outputs, scratch=()):
    held = [] if ORDER.token is None else [ORDER.token]
    unused = len(held)

    def run(*refs):
        body = list(refs[unused:])
        body.pop(len(inputs) + len(outputs))[...] = jnp.zeros((8, 128), F32)
        kernel(*body)

    *results, ORDER.token = pl.pallas_call(
        run,
        grid=grid,
        in_specs=[pl.BlockSpec(memory_space=pltpu.HBM)] * unused + [spec for _, spec in inputs],
        out_specs=[spec for _, spec in outputs] + [whole((8, 128))],
        out_shape=[shape for shape, _ in outputs] + [out(8, 128, dtype=F32)],
        scratch_shapes=list(scratch),
        compiler_params=pltpu.CompilerParams(vmem_limit_bytes=VMEM_LIMIT),
        cost_estimate=pl.CostEstimate(
            flops=int(ORDER.cost * 10**9), bytes_accessed=0, transcendentals=0
        ),
    )(*held, *[value for value, _ in inputs])
    return results


def whole(shape):
    return pl.BlockSpec(shape, lambda *_: (0,) * len(shape))


def columns(shape, offset=0):
    lead = (0,) * (len(shape) - 1)
    return pl.BlockSpec(tuple(shape[:-1]) + (TILE,), lambda i: lead + (i + offset // TILE,))


def out(*shape, dtype=BF16):
    return jax.ShapeDtypeStruct(shape, dtype)


SMEM = pl.BlockSpec(memory_space=pltpu.SMEM)


def mm(a, b):
    return jnp.dot(a, b, preferred_element_type=F32)


def mm_turned(a, b):
    return lax.dot_general(a, b, (((1,), (1,)), ((), ())), preferred_element_type=F32)


PIECES = ((0, 0), (0, 1), (0, 2), (2, 0), (2, 1), (1, 0), (1, 2))
RANKED = [(0, r) for r in range(16)] + [
    (g, r) for g in (1, 2) for line in (0, 3 - g) for r in range(line * 4, line * 4 + 4)
]


def prepare(at, info, cap, held):
    sources, _, tokens = info.shape
    row_of = {(g, r, e): n * held + e for n, (g, r) in enumerate(RANKED) for e in range(held)}
    rows = len(row_of)
    packed, line = held * 4 * cap, 4 * tokens

    def kernel(at_ref, info_ref, pick_ref, key_ref, gate_ref, named_ref):
        for n, (g, r) in enumerate(RANKED):
            block = info_ref[at_ref[r]].astype(F32)
            for e in range(held):
                expert = at_ref[16 + g * held + e].astype(F32)
                hit = block[:8] == expert
                named_ref[n * held + e : n * held + e + 1, :] = jnp.max(
                    jnp.where(hit, 1.0, 0.0), axis=0, keepdims=True
                )
                if g == 0:
                    gate_ref[n * held + e : n * held + e + 1, :] = jnp.sum(
                        jnp.where(hit, block[8:], 0.0), axis=0, keepdims=True
                    )
        named = named_ref[...]
        first = lax.broadcasted_iota(jnp.int32, (tokens, tokens), 0)
        second = lax.broadcasted_iota(jnp.int32, (tokens, tokens), 1)
        before = jnp.where(first < second, 1.0, 0.0).astype(BF16)
        key = jnp.where(named > 0.5, mm(named.astype(BF16), before), -1.0)
        key_ref[...] = key[: sources * held]
        named_ref[...] = key
        slot = lax.broadcasted_iota(jnp.int32, (cap, tokens), 0).astype(F32)
        none = jnp.zeros((cap, tokens), F32)
        for n, (g, l) in enumerate(PIECES):
            for s in range(4):
                parts = []
                for e in range(held):
                    row = row_of[g, l * 4 + s, e]
                    mine = jnp.where(slot == named_ref[row : row + 1, :], 1.0, 0.0)
                    parts += [mine if t == s else none for t in range(4)]
                pick_ref[n, :, s * tokens : (s + 1) * tokens] = jnp.concatenate(parts, axis=0).astype(BF16)

    return call(
        kernel,
        (1,),
        [(at, SMEM), (info, whole(info.shape))],
        [
            (out(len(PIECES), packed, line), whole((len(PIECES), packed, line))),
            (out(sources * held, tokens, dtype=F32), whole((sources * held, tokens))),
            (out(sources * held, tokens, dtype=F32), whole((sources * held, tokens))),
        ],
        scratch=[pltpu.VMEM((rows, tokens), F32)],
    )


def slot_hits(key_ref, row, cap):
    key = key_ref[row : row + 1, :]
    slot = lax.broadcasted_iota(jnp.int32, (cap, key.shape[1]), 0).astype(F32)
    return slot == key


def turn_hidden(at, key, gate, hidden):
    held, sources, cap, ff = hidden.shape
    block = ff // 8

    def kernel(at_ref, key_ref, gate_ref, hidden_ref, out_ref):
        for e in range(held):
            parts = []
            for r in range(sources):
                row = r * held + e
                weight = jnp.sum(
                    jnp.where(slot_hits(key_ref, row, cap), gate_ref[row : row + 1, :], 0.0),
                    axis=1,
                    keepdims=True,
                )
                parts.append(hidden_ref[e, at_ref[r]].astype(F32) * weight)
            turned = jnp.concatenate(parts, axis=0).T.astype(BF16)
            for b in range(8):
                out_ref[at_ref[24 + b], e] = turned[b * block : (b + 1) * block]

    shape = (8, held, block, sources * cap)
    return call(
        kernel,
        (1,),
        [(at, SMEM), (key, whole(key.shape)), (gate, whole(gate.shape)), (hidden, whole(hidden.shape))],
        [(out(*shape), whole(shape))],
    )[0]


def share(info, sources):
    def kernel(info_ref, out_ref):
        out_ref[...] = jnp.broadcast_to(info_ref[...].astype(BF16)[None], out_ref.shape)

    shape = (sources,) + info.shape
    return call(kernel, (1,), [(info, whole(info.shape))], [(out(*shape), whole(shape))])[0]


def own_rows(d_output, offset, size):
    tokens = d_output.shape[0]

    def kernel(in_ref, out_ref):
        out_ref[...] = in_ref[...]

    return call(
        kernel,
        (size // TILE,),
        [(d_output, columns(d_output.shape, offset))],
        [(out(tokens, size), columns((tokens, size)))],
    )[0]


def join(d_output, offset, pieces):
    tokens, size = d_output.shape[0], pieces[0][0].shape[1]

    def spec(at):
        return pl.BlockSpec((tokens, TILE), lambda i: (at, i))

    def kernel(*refs):
        for n, ref in enumerate(refs[:-1]):
            refs[-1][n * tokens : (n + 1) * tokens, :] = ref[...]

    shape = (tokens * (1 + len(pieces)), size)
    return call(
        kernel,
        (size // TILE,),
        [(d_output, columns(d_output.shape, offset))] + [(b, spec(at)) for b, at in pieces],
        [(out(*shape), columns(shape))],
    )[0]


def pack(rows, far, pick, held, parity):
    line, size = rows.shape
    count = pick.shape[1]
    per = count // held
    shape = (held, 2 * per, size)
    near, there = 1 + parity, 2 - parity

    places = [(group, start) for group in (there, 0) for start in (0, near)]

    def kernel(rows_ref, far_ref, *refs):
        picks, (here_ref, there_ref) = refs[:4], refs[4:]
        for k, pick_ref in enumerate(picks):
            chosen = mm(pick_ref[0], (rows_ref, far_ref)[k % 2][...]).astype(BF16)
            target, n = (there_ref, here_ref)[k // 2], k % 2
            for e in range(held):
                target[e, n * per : (n + 1) * per, :] = chosen[e * per : (e + 1) * per]

    def piece(place):
        at = PIECES.index(place)
        return pl.BlockSpec((1, count, line), lambda i: (at, 0, 0))

    return call(
        kernel,
        (size // TILE,),
        [(rows, columns(rows.shape)), (far, columns(far.shape))]
        + [(pick, piece(place)) for place in places],
        [(out(*shape), columns(shape)), (out(*shape), columns(shape))],
    )


def collect(here, came, turned, parity):
    held, half, size = here.shape
    block, total = turned.shape[2:]
    per = half // 2
    places = ((0, 1), (2, 3)) if parity == 0 else ((0, 2), (1, 3))

    def kernel(here_ref, came_ref, turned_ref, slots_ref, other_ref):
        for e in range(held):
            for ref, lines in zip((here_ref, came_ref), places):
                for n, at in enumerate(lines):
                    slots_ref[e, at * per : (at + 1) * per, :] = ref[e, n * per : (n + 1) * per]
            left = turned_ref[:, e].reshape(4 * block, total)
            product = mm(left, slots_ref[e])
            for n in range(4):
                other_ref[n, e] = product[n * block : (n + 1) * block].astype(BF16)

    return call(
        kernel,
        (size // TILE,),
        [
            (here, columns(here.shape)),
            (came, columns(came.shape)),
            (turned, pl.BlockSpec((4, held, block, total), lambda i: (1, 0, 0, 0))),
        ],
        [
            (out(held, total, size), columns((held, total, size))),
            (out(4, held, block, size), columns((4, held, block, size))),
        ],
    )


def own_product(slots, turned):
    held, total, size = slots.shape
    block = turned.shape[2]

    def kernel(slots_ref, turned_ref, mine_ref):
        for e in range(held):
            product = mm(turned_ref[:, e].reshape(4 * block, total), slots_ref[e])
            for n in range(4):
                mine_ref[n, e] = product[n * block : (n + 1) * block].astype(BF16)

    return call(
        kernel,
        (size // TILE,),
        [
            (slots, columns(slots.shape)),
            (turned, pl.BlockSpec((4, held, block, total), lambda i: (0, 0, 0, 0))),
        ],
        [(out(4, held, block, size), columns((4, held, block, size)))],
    )[0]


def add_parts(terms):
    shape = (len(terms),) + terms[0][0][0].shape[1:]
    flat = [term for group in terms for term in group]
    width = len(terms[0])

    def spec(at):
        return pl.BlockSpec((1,) + shape[1:-1] + (TILE,), lambda i: (at, 0, 0, i))

    def kernel(*refs):
        for n in range(len(terms)):
            value = 0.0
            for ref in refs[n * width : (n + 1) * width]:
                value = value + ref[0].astype(F32)
            refs[-1][n] = value.astype(BF16)

    return call(
        kernel,
        (shape[-1] // TILE,),
        [(array, spec(at)) for array, at in flat],
        [(out(*shape), columns(shape))],
    )[0]


def finish(parts, width):
    _, held, block, _ = parts[0][0].shape
    counts = [group[0].shape[3] // DEEP for group in parts]
    starts = [sum(counts[:n]) for n in range(len(counts))]
    terms = len(parts[0])

    def kernel(*refs):
        step = pl.program_id(0)
        for n, (start, count) in enumerate(zip(starts, counts)):

            @pl.when((step >= start) & (step < start + count))
            def _(n=n):
                value = 0.0
                for ref in refs[n * terms : (n + 1) * terms]:
                    value = value + ref[0].astype(F32)
                refs[-1][...] = value.astype(BF16)

    def spec(start, count):
        return pl.BlockSpec(
            (1, held, block, DEEP),
            lambda i: (0, 0, 0, jnp.minimum(jnp.maximum(i - start, 0), count - 1)),
        )

    shape = (held, block, width)
    return call(
        kernel,
        (width // DEEP,),
        [(part, spec(a, c)) for group, a, c in zip(parts, starts, counts) for part in group],
        [(out(*shape), pl.BlockSpec((held, block, DEEP), lambda i: (0, 0, i)))],
    )[0]


def chunk_specs(halves, offset, ff):
    rows = halves[0].shape[1]
    counts = [h.shape[2] // DEEP for h in halves]
    starts = [sum(counts[:n]) for n in range(len(halves))]

    def spec(start, count):
        return pl.BlockSpec(
            (1, rows, DEEP), lambda e, i: (e, 0, jnp.minimum(jnp.maximum(i - start, 0), count - 1))
        )

    specs = [spec(a, b) for a, b in zip(starts, counts)]
    return counts, starts, specs, pl.BlockSpec((1, ff, DEEP), lambda e, i: (e, 0, i + offset // DEEP))


def add_chunks(refs, starts, counts, lines, w_ref, sum_ref):
    step = pl.program_id(1)
    for n, (ref, start, count) in enumerate(zip(refs, starts, counts)):

        @pl.when((step >= start) & (step < start + count))
        def _(n=n, ref=ref):
            product = mm_turned(ref[0], w_ref[0])
            per = product.shape[0] // 2
            for k, line in enumerate(lines[n % 2]):
                sum_ref[line * per : (line + 1) * per, :] += product[k * per : (k + 1) * per]


HERE = ((0, 1), (0, 2))
CAME = ((2, 3), (1, 3))


def hidden_sums(halves, offset, w_down):
    held, rows, _ = halves[0].shape
    ff, total = w_down.shape[1], 2 * rows
    counts, starts, specs, w_spec = chunk_specs(halves, offset, ff)

    def kernel(*refs):
        w_ref, sum_ref, acc_ref = refs[len(halves) :]

        @pl.when(pl.program_id(1) == 0)
        def _():
            acc_ref[...] = jnp.zeros_like(acc_ref)

        add_chunks(refs, starts, counts, HERE, w_ref, acc_ref)

        @pl.when(pl.program_id(1) == sum(counts) - 1)
        def _():
            sum_ref[0] = acc_ref[...]

    return call(
        kernel,
        (held, sum(counts)),
        list(zip(halves, specs)) + [(w_down, w_spec)],
        [(out(held, total, ff, dtype=F32), pl.BlockSpec((1, total, ff), lambda e, i: (e, 0, 0)))],
        scratch=[pltpu.VMEM((total, ff), F32)],
    )[0]


def hidden_end(at, key, gate, hidden, sums, halves, w_down):
    held, sources, cap, ff = hidden.shape
    total = sums[0].shape[1]
    tokens = key.shape[1]
    counts, starts, specs, w_spec = chunk_specs(halves, 0, ff)

    def kernel(at_ref, key_ref, gate_ref, hidden_ref, *refs):
        sums_refs, refs = refs[: len(sums)], refs[len(sums) :]
        w_ref, d_hidden_ref, grad_ref, acc_ref = refs[len(halves) :]

        @pl.when(pl.program_id(1) == 0)
        def _():
            acc_ref[...] = sum(ref[0] for ref in sums_refs)

        add_chunks(refs, starts, counts, CAME, w_ref, acc_ref)

        def end(e):
            for r in range(sources):
                row = r * held + e
                hits = slot_hits(key_ref, row, cap)
                weight = jnp.sum(
                    jnp.where(hits, gate_ref[row : row + 1, :], 0.0), axis=1, keepdims=True
                )
                value = acc_ref[r * cap : (r + 1) * cap, :]
                place = at_ref[r]
                d_hidden_ref[0, place] = (value * weight).astype(BF16)
                dots = jnp.sum(value * hidden_ref[0, place].astype(F32), axis=1, keepdims=True)
                grad_ref[place, e : e + 1, :] = jnp.sum(
                    jnp.where(hits, dots, 0.0), axis=0, keepdims=True
                )

        for e in range(held):

            @pl.when((pl.program_id(1) == sum(counts) - 1) & (pl.program_id(0) == e))
            def _(e=e):
                end(e)

    by_expert = pl.BlockSpec((1, sources, cap, ff), lambda e, i: (e, 0, 0, 0))
    return call(
        kernel,
        (held, sum(counts)),
        [
            (at, SMEM),
            (key, whole(key.shape)),
            (gate, whole(gate.shape)),
            (hidden, by_expert),
        ]
        + [(part, pl.BlockSpec((1, total, ff), lambda e, i: (e, 0, 0))) for part in sums]
        + list(zip(halves, specs))
        + [(w_down, w_spec)],
        [
            (out(*hidden.shape), by_expert),
            (out(sources, held, tokens, dtype=F32), whole((sources, held, tokens))),
        ],
        scratch=[pltpu.VMEM((total, ff), F32)],
    )


def shards(d_output, gate_values, routes, hidden_saved, w_down):
    ORDER.token = None
    tokens, width = d_output.shape
    hidden = hidden_saved[0]
    held, sources, cap, ff = hidden.shape

    section, group = lax.axis_index("section"), lax.axis_index("expert")
    z, core, y, x = section // 2, section % 2, group // 4, group % 4
    masks = jnp.stack([0 * core, 1 + 2 * core, 3 - 2 * core, 0 * core + 2])
    first_at = jnp.where(core == 0, x, y) ^ masks
    second_at = jnp.where(core == 0, y, x) ^ masks
    up_first, up_second = jnp.where(core == 0, 1, 4), jnp.where(core == 0, 4, 1)
    source_at = (second_at[:, None] * up_second + first_at[None, :] * up_first).reshape(-1)
    group_at = second_at[:4] * up_second + first_at[0] * up_first
    experts = (group_at[:, None] * held + jnp.arange(held)[None, :]).reshape(-1)
    section_at = jnp.arange(8)
    met = (section_at // 2) ^ z
    place = jnp.where(met == 2, 3, jnp.where(met == 0, 0, jnp.where((met == 1) == (section_at % 2 == 0), 2, 1)))
    is_mine = section_at % 2 == core
    at = jnp.concatenate([source_at, experts, jnp.where(is_mine, place, 4 + place)]).astype(jnp.int32)

    offsets = [sum(CHUNKS[:n]) for n in range(len(CHUNKS))]
    info = jnp.concatenate([routes.astype(F32), gate_values.astype(F32)], axis=1).T
    count = len(CHUNKS)
    one, two, rows, far, here, came, slots = ([None] * count for _ in range(7))
    hidden_parts = [None] * (count // 2)
    got, mine, passed, more = ([None] * count for _ in range(4))
    for n in range(2):
        own = d_output[:, offsets[n] : offsets[n] + CHUNKS[n]]
        one[n] = send(own, along("first", 0, n % 2))

    for step in PLAN:
        kind, n = step[0], int(step[1:2].strip("-") or 0)
        parity = n % 2
        ORDER.cost = 0 if step.endswith("-") else 20
        if kind == "o":
            one[n] = send(own_rows(d_output, offsets[n], CHUNKS[n]), along("first", 0, parity))
        elif kind == "I":
            all_info = lax.all_to_all(share(info, sources), "expert", 0, 0, tiled=True)
        elif kind == "P":
            pick, key, gate = prepare(at, all_info, cap, held)
        elif kind == "T":
            turned = turn_hidden(at, key, gate, hidden)
        elif kind == "a":
            two[n] = send(join(d_output, offsets[n], [(one[n], 0)]), along("first", 1, parity))
        elif kind == "r":
            came_rows = [(one[n], 0), (two[n], 0), (two[n], 1)]
            if parity == 1:
                came_rows = [(two[n], 0), (one[n], 0), (two[n], 1)]
            rows[n] = join(d_output, offsets[n], came_rows)
            far[n] = send(rows[n], along("second", 0, parity))
        elif kind == "p":
            here[n], there = pack(rows[n], far[n], pick, held, parity)
            came[n] = send(there, along("second", 1, parity))
        elif kind == "w":
            slots[n], other = collect(here[n], came[n], turned, parity)
            got[n] = send(other, SWAP)
        elif kind == "m":
            mine[n] = own_product(slots[n], turned)
        elif kind == "s":
            sums = add_parts([[(mine[n], k), (got[n], k)] for k in (2 - parity, 3)])
            passed[n] = send(sums, along("z", 0, parity))
        elif kind == "t":
            sums = add_parts([[(mine[n], 1 + parity), (got[n], 1 + parity), (passed[n], 1)]])
            more[n] = send(sums, along("z", 1, parity))
        elif kind == "e":
            parts = [(mine[k], got[k], passed[k], more[k]) for k in range(count)]
            d_weight = finish(parts, width)
        elif kind == "h":
            hidden_parts[n] = hidden_sums(here[2 * n : 2 * n + 2], offsets[2 * n], w_down)
        elif kind == "H":
            d_hidden, token_grad = hidden_end(at, key, gate, hidden, hidden_parts, came, w_down)
    returned = lax.all_to_all(token_grad, "expert", 0, 0, tiled=True).reshape(-1, tokens)
    chosen = routes.T[None] == jnp.arange(sources * held)[:, None, None]
    d_gate = jnp.sum(jnp.where(chosen, returned[:, None, :], 0.0), axis=0).T
    return (d_hidden[None], d_weight, d_gate)


def solution(mesh):
    placed = (
        P(("section", "expert"), None),
        P(("section", "expert"), None),
        P(("section", "expert"), None),
        P("section", "expert", None, None, None),
        P("expert", None, None),
    )
    return jax.shard_map(
        shards,
        mesh=mesh,
        in_specs=placed,
        out_specs=(
            P("section", "expert", None, None, None),
            P("expert", "section", None),
            P(("section", "expert"), None),
        ),
        check_vma=False,
    )
```

```python
import jax
import jax.numpy as jnp
from jax import lax
from jax.experimental import pallas as pl
from jax.experimental.pallas import tpu as pltpu
from jax.sharding import PartitionSpec as P

AXES = ("section", "expert")
CHUNKS = (1024, 1024, 1024, 1024)
TILE = 1024
DEEP = 1024
VMEM_LIMIT = 20 * 1024 * 1024
END_LIMIT = 46 * 1024 * 1024
PLAN = (
    "a0", "a1", "o2-", "o3-", "I-", "r0-", "r1-", "a2", "a3", "P-", "T-", "r2", "r3", "p0",
    "p1", "h0", "p2", "p3", "h1", "w0", "m0", "w1", "m1", "s0", "s1", "w2", "w3", "m2", "m3",
    "s2", "s3", "H", "t0-", "t1-", "t2-", "t3-", "e",
)
F32, BF16 = jnp.float32, jnp.bfloat16


def moves(move):
    pairs = []
    for z in range(4):
        for core in range(2):
            for y in range(4):
                for x in range(4):
                    tz, tcore, ty, tx = move(z, core, y, x)
                    pairs.append(
                        (
                            ((z * 2 + core) * 4 + y) * 4 + x,
                            ((tz % 4 * 2 + tcore) * 4 + ty % 4) * 4 + tx % 4,
                        )
                    )
    return pairs


MEET = ((1, 3), (3, 1))


def along(axis, step, parity=0):
    def move(z, core, y, x):
        mask = MEET[core][(step + parity) % 2]
        if axis == "z":
            return (z ^ mask, core, y, x)
        if (axis == "first") == (core == 0):
            return (z, core, y, x ^ mask)
        return (z, core, y ^ mask, x)

    return moves(move)


SWAP = moves(lambda z, core, y, x: (z, 1 - core, y, x))


def send(value, pairs):
    return lax.ppermute(value, AXES, pairs)


class Order:
    def __init__(self):
        self.token = None
        self.cost = 0
        self.room = VMEM_LIMIT


ORDER = Order()


def call(kernel, grid, inputs, outputs, scratch=()):
    held = [] if ORDER.token is None else [ORDER.token]
    unused = len(held)

    def run(*refs):
        body = list(refs[unused:])
        body.pop(len(inputs) + len(outputs))[...] = jnp.zeros((8, 128), F32)
        kernel(*body)

    *results, ORDER.token = pl.pallas_call(
        run,
        grid=grid,
        in_specs=[pl.BlockSpec(memory_space=pltpu.HBM)] * unused + [spec for _, spec in inputs],
        out_specs=[spec for _, spec in outputs] + [whole((8, 128))],
        out_shape=[shape for shape, _ in outputs] + [out(8, 128, dtype=F32)],
        scratch_shapes=list(scratch),
        compiler_params=pltpu.CompilerParams(vmem_limit_bytes=ORDER.room),
        cost_estimate=pl.CostEstimate(
            flops=int(ORDER.cost * 10**9), bytes_accessed=0, transcendentals=0
        ),
    )(*held, *[value for value, _ in inputs])
    return results


def whole(shape):
    return pl.BlockSpec(shape, lambda *_: (0,) * len(shape))


def columns(shape, offset=0):
    lead = (0,) * (len(shape) - 1)
    return pl.BlockSpec(tuple(shape[:-1]) + (TILE,), lambda i: lead + (i + offset // TILE,))


def out(*shape, dtype=BF16):
    return jax.ShapeDtypeStruct(shape, dtype)


SMEM = pl.BlockSpec(memory_space=pltpu.SMEM)


def mm(a, b):
    return jnp.dot(a, b, preferred_element_type=F32)


def mm_turned(a, b):
    return lax.dot_general(a, b, (((1,), (1,)), ((), ())), preferred_element_type=F32)


PIECES = ((0, 0), (0, 1), (0, 2), (2, 0), (2, 1), (1, 0), (1, 2))
RANKED = [(0, r) for r in range(16)] + [
    (g, r) for g in (1, 2) for line in (0, 3 - g) for r in range(line * 4, line * 4 + 4)
]


def prepare(at, info, cap, held):
    sources, _, tokens = info.shape
    row_of = {(g, r, e): n * held + e for n, (g, r) in enumerate(RANKED) for e in range(held)}
    rows = len(row_of)
    packed, line = held * 4 * cap, 4 * tokens

    def kernel(at_ref, info_ref, pick_ref, key_ref, gate_ref, named_ref):
        for n, (g, r) in enumerate(RANKED):
            block = info_ref[at_ref[r]].astype(F32)
            for e in range(held):
                expert = at_ref[16 + g * held + e].astype(F32)
                hit = block[:8] == expert
                named_ref[n * held + e : n * held + e + 1, :] = jnp.max(
                    jnp.where(hit, 1.0, 0.0), axis=0, keepdims=True
                )
                if g == 0:
                    gate_ref[n * held + e : n * held + e + 1, :] = jnp.sum(
                        jnp.where(hit, block[8:], 0.0), axis=0, keepdims=True
                    )
        named = named_ref[...]
        first = lax.broadcasted_iota(jnp.int32, (tokens, tokens), 0)
        second = lax.broadcasted_iota(jnp.int32, (tokens, tokens), 1)
        before = jnp.where(first < second, 1.0, 0.0).astype(BF16)
        key = jnp.where(named > 0.5, mm(named.astype(BF16), before), -1.0)
        key_ref[...] = key[: sources * held]
        named_ref[...] = key
        slot = lax.broadcasted_iota(jnp.int32, (cap, tokens), 0).astype(F32)
        none = jnp.zeros((cap, tokens), F32)
        for n, (g, l) in enumerate(PIECES):
            for s in range(4):
                parts = []
                for e in range(held):
                    row = row_of[g, l * 4 + s, e]
                    mine = jnp.where(slot == named_ref[row : row + 1, :], 1.0, 0.0)
                    parts += [mine if t == s else none for t in range(4)]
                pick_ref[n, :, s * tokens : (s + 1) * tokens] = jnp.concatenate(parts, axis=0).astype(BF16)

    return call(
        kernel,
        (1,),
        [(at, SMEM), (info, whole(info.shape))],
        [
            (out(len(PIECES), packed, line), whole((len(PIECES), packed, line))),
            (out(sources * held, tokens, dtype=F32), whole((sources * held, tokens))),
            (out(sources * held, tokens, dtype=F32), whole((sources * held, tokens))),
        ],
        scratch=[pltpu.VMEM((rows, tokens), F32)],
    )


def slot_hits(key_ref, row, cap):
    key = key_ref[row : row + 1, :]
    slot = lax.broadcasted_iota(jnp.int32, (cap, key.shape[1]), 0).astype(F32)
    return slot == key


def turn_hidden(at, key, gate, hidden):
    held, sources, cap, ff = hidden.shape
    block = ff // 8

    def kernel(at_ref, key_ref, gate_ref, hidden_ref, out_ref):
        for e in range(held):
            parts = []
            for r in range(sources):
                row = r * held + e
                weight = jnp.sum(
                    jnp.where(slot_hits(key_ref, row, cap), gate_ref[row : row + 1, :], 0.0),
                    axis=1,
                    keepdims=True,
                )
                parts.append(hidden_ref[e, at_ref[r]].astype(F32) * weight)
            turned = jnp.concatenate(parts, axis=0).T.astype(BF16)
            for b in range(8):
                out_ref[at_ref[24 + b], e] = turned[b * block : (b + 1) * block]

    shape = (8, held, block, sources * cap)
    return call(
        kernel,
        (1,),
        [(at, SMEM), (key, whole(key.shape)), (gate, whole(gate.shape)), (hidden, whole(hidden.shape))],
        [(out(*shape), whole(shape))],
    )[0]


def share(info, sources):
    def kernel(info_ref, out_ref):
        out_ref[...] = jnp.broadcast_to(info_ref[...].astype(BF16)[None], out_ref.shape)

    shape = (sources,) + info.shape
    return call(kernel, (1,), [(info, whole(info.shape))], [(out(*shape), whole(shape))])[0]


def own_rows(d_output, offset, size):
    tokens = d_output.shape[0]

    def kernel(in_ref, out_ref):
        out_ref[...] = in_ref[...]

    return call(
        kernel,
        (size // TILE,),
        [(d_output, columns(d_output.shape, offset))],
        [(out(tokens, size), columns((tokens, size)))],
    )[0]


def join(d_output, offset, pieces):
    tokens, size = d_output.shape[0], pieces[0][0].shape[1]

    def spec(at):
        return pl.BlockSpec((tokens, TILE), lambda i: (at, i))

    def kernel(*refs):
        for n, ref in enumerate(refs[:-1]):
            refs[-1][n * tokens : (n + 1) * tokens, :] = ref[...]

    shape = (tokens * (1 + len(pieces)), size)
    return call(
        kernel,
        (size // TILE,),
        [(d_output, columns(d_output.shape, offset))] + [(b, spec(at)) for b, at in pieces],
        [(out(*shape), columns(shape))],
    )[0]


def pack(rows, far, pick, held, parity):
    line, size = rows.shape
    count = pick.shape[1]
    per = count // held
    shape = (held, 2 * per, size)
    near, there = 1 + parity, 2 - parity

    places = [(group, start) for group in (there, 0) for start in (0, near)]

    def kernel(rows_ref, far_ref, *refs):
        picks, (here_ref, there_ref) = refs[:4], refs[4:]
        for k, pick_ref in enumerate(picks):
            chosen = mm(pick_ref[0], (rows_ref, far_ref)[k % 2][...]).astype(BF16)
            target, n = (there_ref, here_ref)[k // 2], k % 2
            for e in range(held):
                target[e, n * per : (n + 1) * per, :] = chosen[e * per : (e + 1) * per]

    def piece(place):
        at = PIECES.index(place)
        return pl.BlockSpec((1, count, line), lambda i: (at, 0, 0))

    return call(
        kernel,
        (size // TILE,),
        [(rows, columns(rows.shape)), (far, columns(far.shape))]
        + [(pick, piece(place)) for place in places],
        [(out(*shape), columns(shape)), (out(*shape), columns(shape))],
    )


def collect(here, came, turned, parity):
    held, half, size = here.shape
    block, total = turned.shape[2:]
    per = half // 2
    places = ((0, 1), (2, 3)) if parity == 0 else ((0, 2), (1, 3))

    def kernel(here_ref, came_ref, turned_ref, slots_ref, other_ref):
        for e in range(held):
            for ref, lines in zip((here_ref, came_ref), places):
                for n, at in enumerate(lines):
                    slots_ref[e, at * per : (at + 1) * per, :] = ref[e, n * per : (n + 1) * per]
            left = turned_ref[:, e].reshape(4 * block, total)
            product = mm(left, slots_ref[e])
            for n in range(4):
                other_ref[n, e] = product[n * block : (n + 1) * block].astype(BF16)

    return call(
        kernel,
        (size // TILE,),
        [
            (here, columns(here.shape)),
            (came, columns(came.shape)),
            (turned, pl.BlockSpec((4, held, block, total), lambda i: (1, 0, 0, 0))),
        ],
        [
            (out(held, total, size), columns((held, total, size))),
            (out(4, held, block, size), columns((4, held, block, size))),
        ],
    )


def own_product(slots, turned):
    held, total, size = slots.shape
    block = turned.shape[2]

    def kernel(slots_ref, turned_ref, mine_ref):
        for e in range(held):
            product = mm(turned_ref[:, e].reshape(4 * block, total), slots_ref[e])
            for n in range(4):
                mine_ref[n, e] = product[n * block : (n + 1) * block].astype(BF16)

    return call(
        kernel,
        (size // TILE,),
        [
            (slots, columns(slots.shape)),
            (turned, pl.BlockSpec((4, held, block, total), lambda i: (0, 0, 0, 0))),
        ],
        [(out(4, held, block, size), columns((4, held, block, size)))],
    )[0]


def add_parts(terms):
    shape = (len(terms),) + terms[0][0][0].shape[1:]
    flat = [term for group in terms for term in group]
    width = len(terms[0])

    def spec(at):
        return pl.BlockSpec((1,) + shape[1:-1] + (TILE,), lambda i: (at, 0, 0, i))

    def kernel(*refs):
        for n in range(len(terms)):
            value = 0.0
            for ref in refs[n * width : (n + 1) * width]:
                value = value + ref[0].astype(F32)
            refs[-1][n] = value.astype(BF16)

    return call(
        kernel,
        (shape[-1] // TILE,),
        [(array, spec(at)) for array, at in flat],
        [(out(*shape), columns(shape))],
    )[0]


def finish(parts, width):
    _, held, block, _ = parts[0][0].shape
    counts = [group[0].shape[3] // DEEP for group in parts]
    starts = [sum(counts[:n]) for n in range(len(counts))]
    terms = len(parts[0])

    def kernel(*refs):
        step = pl.program_id(0)
        for n, (start, count) in enumerate(zip(starts, counts)):

            @pl.when((step >= start) & (step < start + count))
            def _(n=n):
                value = 0.0
                for ref in refs[n * terms : (n + 1) * terms]:
                    value = value + ref[0].astype(F32)
                refs[-1][...] = value.astype(BF16)

    def spec(start, count):
        return pl.BlockSpec(
            (1, held, block, DEEP),
            lambda i: (0, 0, 0, jnp.minimum(jnp.maximum(i - start, 0), count - 1)),
        )

    shape = (held, block, width)
    return call(
        kernel,
        (width // DEEP,),
        [(part, spec(a, c)) for group, a, c in zip(parts, starts, counts) for part in group],
        [(out(*shape), pl.BlockSpec((held, block, DEEP), lambda i: (0, 0, i)))],
    )[0]


def chunk_specs(halves, offset, ff):
    rows = halves[0].shape[1]
    counts = [h.shape[2] // DEEP for h in halves]
    starts = [sum(counts[:n]) for n in range(len(halves))]

    def spec(start, count):
        return pl.BlockSpec(
            (1, rows, DEEP), lambda e, i: (e, 0, jnp.minimum(jnp.maximum(i - start, 0), count - 1))
        )

    specs = [spec(a, b) for a, b in zip(starts, counts)]
    return counts, starts, specs, pl.BlockSpec((1, ff, DEEP), lambda e, i: (e, 0, i + offset // DEEP))


def add_chunks(refs, starts, counts, lines, w_ref, sum_ref):
    step = pl.program_id(1)
    for n, (ref, start, count) in enumerate(zip(refs, starts, counts)):

        @pl.when((step >= start) & (step < start + count))
        def _(n=n, ref=ref):
            product = mm_turned(ref[0], w_ref[0])
            per = product.shape[0] // 2
            for k, line in enumerate(lines[n % 2]):
                sum_ref[line * per : (line + 1) * per, :] += product[k * per : (k + 1) * per]


HERE = ((0, 1), (0, 2))
CAME = ((2, 3), (1, 3))


def hidden_sums(halves, offset, w_down):
    held, rows, _ = halves[0].shape
    ff, total = w_down.shape[1], 2 * rows
    counts, starts, specs, w_spec = chunk_specs(halves, offset, ff)

    def kernel(*refs):
        w_ref, sum_ref, acc_ref = refs[len(halves) :]

        @pl.when(pl.program_id(1) == 0)
        def _():
            acc_ref[...] = jnp.zeros_like(acc_ref)

        add_chunks(refs, starts, counts, HERE, w_ref, acc_ref)

        @pl.when(pl.program_id(1) == sum(counts) - 1)
        def _():
            sum_ref[0] = acc_ref[...]

    return call(
        kernel,
        (held, sum(counts)),
        list(zip(halves, specs)) + [(w_down, w_spec)],
        [(out(held, total, ff, dtype=F32), pl.BlockSpec((1, total, ff), lambda e, i: (e, 0, 0)))],
        scratch=[pltpu.VMEM((total, ff), F32)],
    )[0]


def hidden_end(at, key, gate, hidden, sums, halves, w_down):
    held, sources, cap, ff = hidden.shape
    total = sums[0].shape[1]
    tokens = key.shape[1]
    counts, starts, specs, w_spec = chunk_specs(halves, 0, ff)

    def kernel(at_ref, key_ref, gate_ref, hidden_ref, *refs):
        sums_refs, refs = refs[: len(sums)], refs[len(sums) :]
        w_ref, d_hidden_ref, grad_ref, acc_ref = refs[len(halves) :]

        @pl.when(pl.program_id(1) == 0)
        def _():
            acc_ref[...] = sum(ref[0] for ref in sums_refs)

        add_chunks(refs, starts, counts, CAME, w_ref, acc_ref)

        def end(e):
            for r in range(sources):
                row = r * held + e
                hits = slot_hits(key_ref, row, cap)
                weight = jnp.sum(
                    jnp.where(hits, gate_ref[row : row + 1, :], 0.0), axis=1, keepdims=True
                )
                value = acc_ref[r * cap : (r + 1) * cap, :]
                place = at_ref[r]
                d_hidden_ref[0, place] = (value * weight).astype(BF16)
                dots = jnp.sum(value * hidden_ref[0, place].astype(F32), axis=1, keepdims=True)
                grad_ref[place, e : e + 1, :] = jnp.sum(
                    jnp.where(hits, dots, 0.0), axis=0, keepdims=True
                )

        for e in range(held):

            @pl.when((pl.program_id(1) == sum(counts) - 1) & (pl.program_id(0) == e))
            def _(e=e):
                end(e)

    by_expert = pl.BlockSpec((1, sources, cap, ff), lambda e, i: (e, 0, 0, 0))
    return call(
        kernel,
        (held, sum(counts)),
        [
            (at, SMEM),
            (key, whole(key.shape)),
            (gate, whole(gate.shape)),
            (hidden, by_expert),
        ]
        + [(part, pl.BlockSpec((1, total, ff), lambda e, i: (e, 0, 0))) for part in sums]
        + list(zip(halves, specs))
        + [(w_down, w_spec)],
        [
            (out(*hidden.shape), by_expert),
            (out(sources, held, tokens, dtype=F32), whole((sources, held, tokens))),
        ],
        scratch=[pltpu.VMEM((total, ff), F32)],
    )


def shards(d_output, gate_values, routes, hidden_saved, w_down):
    ORDER.token = None
    tokens, width = d_output.shape
    hidden = hidden_saved[0]
    held, sources, cap, ff = hidden.shape

    section, group = lax.axis_index("section"), lax.axis_index("expert")
    z, core, y, x = section // 2, section % 2, group // 4, group % 4
    masks = jnp.stack([0 * core, 1 + 2 * core, 3 - 2 * core, 0 * core + 2])
    first_at = jnp.where(core == 0, x, y) ^ masks
    second_at = jnp.where(core == 0, y, x) ^ masks
    up_first, up_second = jnp.where(core == 0, 1, 4), jnp.where(core == 0, 4, 1)
    source_at = (second_at[:, None] * up_second + first_at[None, :] * up_first).reshape(-1)
    group_at = second_at[:4] * up_second + first_at[0] * up_first
    experts = (group_at[:, None] * held + jnp.arange(held)[None, :]).reshape(-1)
    section_at = jnp.arange(8)
    met = (section_at // 2) ^ z
    place = jnp.where(met == 2, 3, jnp.where(met == 0, 0, jnp.where((met == 1) == (section_at % 2 == 0), 2, 1)))
    is_mine = section_at % 2 == core
    at = jnp.concatenate([source_at, experts, jnp.where(is_mine, place, 4 + place)]).astype(jnp.int32)

    offsets = [sum(CHUNKS[:n]) for n in range(len(CHUNKS))]
    info = jnp.concatenate([routes.astype(F32), gate_values.astype(F32)], axis=1).T
    count = len(CHUNKS)
    one, two, rows, far, here, came, slots = ([None] * count for _ in range(7))
    hidden_parts = [None] * (count // 2)
    got, mine, passed, more = ([None] * count for _ in range(4))
    for n in range(2):
        own = d_output[:, offsets[n] : offsets[n] + CHUNKS[n]]
        one[n] = send(own, along("first", 0, n % 2))

    for step in PLAN:
        kind, n = step[0], int(step[1:2].strip("-") or 0)
        parity = n % 2
        ORDER.room = END_LIMIT if kind == "H" else VMEM_LIMIT
        ORDER.cost = 0 if step.endswith("-") else 20
        if kind == "o":
            one[n] = send(own_rows(d_output, offsets[n], CHUNKS[n]), along("first", 0, parity))
        elif kind == "I":
            all_info = lax.all_to_all(share(info, sources), "expert", 0, 0, tiled=True)
        elif kind == "P":
            pick, key, gate = prepare(at, all_info, cap, held)
        elif kind == "T":
            turned = turn_hidden(at, key, gate, hidden)
        elif kind == "a":
            two[n] = send(join(d_output, offsets[n], [(one[n], 0)]), along("first", 1, parity))
        elif kind == "r":
            came_rows = [(one[n], 0), (two[n], 0), (two[n], 1)]
            if parity == 1:
                came_rows = [(two[n], 0), (one[n], 0), (two[n], 1)]
            rows[n] = join(d_output, offsets[n], came_rows)
            far[n] = send(rows[n], along("second", 0, parity))
        elif kind == "p":
            here[n], there = pack(rows[n], far[n], pick, held, parity)
            came[n] = send(there, along("second", 1, parity))
        elif kind == "w":
            slots[n], other = collect(here[n], came[n], turned, parity)
            got[n] = send(other, SWAP)
        elif kind == "m":
            mine[n] = own_product(slots[n], turned)
        elif kind == "s":
            sums = add_parts([[(mine[n], k), (got[n], k)] for k in (2 - parity, 3)])
            passed[n] = send(sums, along("z", 0, parity))
        elif kind == "t":
            sums = add_parts([[(mine[n], 1 + parity), (got[n], 1 + parity), (passed[n], 1)]])
            more[n] = send(sums, along("z", 1, parity))
        elif kind == "e":
            parts = [(mine[k], got[k], passed[k], more[k]) for k in range(count)]
            d_weight = finish(parts, width)
        elif kind == "h":
            hidden_parts[n] = hidden_sums(here[2 * n : 2 * n + 2], offsets[2 * n], w_down)
        elif kind == "H":
            d_hidden, token_grad = hidden_end(at, key, gate, hidden, hidden_parts, came, w_down)
    returned = lax.all_to_all(token_grad, "expert", 0, 0, tiled=True).reshape(-1, tokens)
    chosen = routes.T[None] == jnp.arange(sources * held)[:, None, None]
    d_gate = jnp.sum(jnp.where(chosen, returned[:, None, :], 0.0), axis=0).T
    return (d_hidden[None], d_weight, d_gate)


def solution(mesh):
    placed = (
        P(("section", "expert"), None),
        P(("section", "expert"), None),
        P(("section", "expert"), None),
        P("section", "expert", None, None, None),
        P("expert", None, None),
    )
    return jax.shard_map(
        shards,
        mesh=mesh,
        in_specs=placed,
        out_specs=(
            P("section", "expert", None, None, None),
            P("expert", "section", None),
            P(("section", "expert"), None),
        ),
        check_vma=False,
    )
```

```python
import jax
import jax.numpy as jnp
from jax import lax
from jax.experimental import pallas as pl
from jax.experimental.pallas import tpu as pltpu
from jax.sharding import PartitionSpec as P

AXES = ("section", "expert")
CHUNKS = (1024, 1024, 1024, 1024)
TILE = 1024
DEEP = 1024
VMEM_LIMIT = 20 * 1024 * 1024
END_LIMIT = 46 * 1024 * 1024
PLAN = (
    "a0", "a1", "o2-", "o3-", "I-", "r0-", "r1-", "a2", "a3", "P-", "T-", "r2", "r3", "p0",
    "p1", "h0", "p2", "p3", "h1", "w0", "m0", "w1", "m1", "s0", "s1", "w2", "w3", "m2", "s2",
    "m3", "s3", "H", "t0-", "t1-", "t2-", "t3-", "e",
)
F32, BF16 = jnp.float32, jnp.bfloat16


def moves(move):
    pairs = []
    for z in range(4):
        for core in range(2):
            for y in range(4):
                for x in range(4):
                    tz, tcore, ty, tx = move(z, core, y, x)
                    pairs.append(
                        (
                            ((z * 2 + core) * 4 + y) * 4 + x,
                            ((tz % 4 * 2 + tcore) * 4 + ty % 4) * 4 + tx % 4,
                        )
                    )
    return pairs


MEET = ((1, 3), (3, 1))


def along(axis, step, parity=0):
    def move(z, core, y, x):
        mask = MEET[core][(step + parity) % 2]
        if axis == "z":
            return (z ^ mask, core, y, x)
        if (axis == "first") == (core == 0):
            return (z, core, y, x ^ mask)
        return (z, core, y ^ mask, x)

    return moves(move)


SWAP = moves(lambda z, core, y, x: (z, 1 - core, y, x))


def send(value, pairs):
    return lax.ppermute(value, AXES, pairs)


class Order:
    def __init__(self):
        self.token = None
        self.cost = 0
        self.room = VMEM_LIMIT


ORDER = Order()


def call(kernel, grid, inputs, outputs, scratch=()):
    held = [] if ORDER.token is None else [ORDER.token]
    unused = len(held)

    def run(*refs):
        body = list(refs[unused:])
        body.pop(len(inputs) + len(outputs))[...] = jnp.zeros((8, 128), F32)
        kernel(*body)

    *results, ORDER.token = pl.pallas_call(
        run,
        grid=grid,
        in_specs=[pl.BlockSpec(memory_space=pltpu.HBM)] * unused + [spec for _, spec in inputs],
        out_specs=[spec for _, spec in outputs] + [whole((8, 128))],
        out_shape=[shape for shape, _ in outputs] + [out(8, 128, dtype=F32)],
        scratch_shapes=list(scratch),
        compiler_params=pltpu.CompilerParams(vmem_limit_bytes=ORDER.room),
        cost_estimate=pl.CostEstimate(
            flops=int(ORDER.cost * 10**9), bytes_accessed=0, transcendentals=0
        ),
    )(*held, *[value for value, _ in inputs])
    return results


def whole(shape):
    return pl.BlockSpec(shape, lambda *_: (0,) * len(shape))


def columns(shape, offset=0):
    lead = (0,) * (len(shape) - 1)
    return pl.BlockSpec(tuple(shape[:-1]) + (TILE,), lambda i: lead + (i + offset // TILE,))


def out(*shape, dtype=BF16):
    return jax.ShapeDtypeStruct(shape, dtype)


SMEM = pl.BlockSpec(memory_space=pltpu.SMEM)


def mm(a, b):
    return jnp.dot(a, b, preferred_element_type=F32)


def mm_turned(a, b):
    return lax.dot_general(a, b, (((1,), (1,)), ((), ())), preferred_element_type=F32)


PIECES = ((0, 0), (0, 1), (0, 2), (2, 0), (2, 1), (1, 0), (1, 2))
RANKED = [(0, r) for r in range(16)] + [
    (g, r) for g in (1, 2) for line in (0, 3 - g) for r in range(line * 4, line * 4 + 4)
]


def prepare(at, info, cap, held):
    sources, _, tokens = info.shape
    row_of = {(g, r, e): n * held + e for n, (g, r) in enumerate(RANKED) for e in range(held)}
    rows = len(row_of)
    packed, line = held * 4 * cap, 4 * tokens

    def kernel(at_ref, info_ref, pick_ref, key_ref, gate_ref, named_ref):
        for n, (g, r) in enumerate(RANKED):
            block = info_ref[at_ref[r]].astype(F32)
            for e in range(held):
                expert = at_ref[16 + g * held + e].astype(F32)
                hit = block[:8] == expert
                named_ref[n * held + e : n * held + e + 1, :] = jnp.max(
                    jnp.where(hit, 1.0, 0.0), axis=0, keepdims=True
                )
                if g == 0:
                    gate_ref[n * held + e : n * held + e + 1, :] = jnp.sum(
                        jnp.where(hit, block[8:], 0.0), axis=0, keepdims=True
                    )
        named = named_ref[...]
        first = lax.broadcasted_iota(jnp.int32, (tokens, tokens), 0)
        second = lax.broadcasted_iota(jnp.int32, (tokens, tokens), 1)
        before = jnp.where(first < second, 1.0, 0.0).astype(BF16)
        key = jnp.where(named > 0.5, mm(named.astype(BF16), before), -1.0)
        key_ref[...] = key[: sources * held]
        named_ref[...] = key
        slot = lax.broadcasted_iota(jnp.int32, (cap, tokens), 0).astype(F32)
        none = jnp.zeros((cap, tokens), F32)
        for n, (g, l) in enumerate(PIECES):
            for s in range(4):
                parts = []
                for e in range(held):
                    row = row_of[g, l * 4 + s, e]
                    mine = jnp.where(slot == named_ref[row : row + 1, :], 1.0, 0.0)
                    parts += [mine if t == s else none for t in range(4)]
                pick_ref[n, :, s * tokens : (s + 1) * tokens] = jnp.concatenate(parts, axis=0).astype(BF16)

    return call(
        kernel,
        (1,),
        [(at, SMEM), (info, whole(info.shape))],
        [
            (out(len(PIECES), packed, line), whole((len(PIECES), packed, line))),
            (out(sources * held, tokens, dtype=F32), whole((sources * held, tokens))),
            (out(sources * held, tokens, dtype=F32), whole((sources * held, tokens))),
        ],
        scratch=[pltpu.VMEM((rows, tokens), F32)],
    )


def slot_hits(key_ref, row, cap):
    key = key_ref[row : row + 1, :]
    slot = lax.broadcasted_iota(jnp.int32, (cap, key.shape[1]), 0).astype(F32)
    return slot == key


def turn_hidden(at, key, gate, hidden):
    held, sources, cap, ff = hidden.shape
    block = ff // 8

    def kernel(at_ref, key_ref, gate_ref, hidden_ref, out_ref):
        for e in range(held):
            parts = []
            for r in range(sources):
                row = r * held + e
                weight = jnp.sum(
                    jnp.where(slot_hits(key_ref, row, cap), gate_ref[row : row + 1, :], 0.0),
                    axis=1,
                    keepdims=True,
                )
                parts.append(hidden_ref[e, at_ref[r]].astype(F32) * weight)
            turned = jnp.concatenate(parts, axis=0).T.astype(BF16)
            for b in range(8):
                out_ref[at_ref[24 + b], e] = turned[b * block : (b + 1) * block]

    shape = (8, held, block, sources * cap)
    return call(
        kernel,
        (1,),
        [(at, SMEM), (key, whole(key.shape)), (gate, whole(gate.shape)), (hidden, whole(hidden.shape))],
        [(out(*shape), whole(shape))],
    )[0]


def share(info, sources):
    def kernel(info_ref, out_ref):
        out_ref[...] = jnp.broadcast_to(info_ref[...].astype(BF16)[None], out_ref.shape)

    shape = (sources,) + info.shape
    return call(kernel, (1,), [(info, whole(info.shape))], [(out(*shape), whole(shape))])[0]


def own_rows(d_output, offset, size):
    tokens = d_output.shape[0]

    def kernel(in_ref, out_ref):
        out_ref[...] = in_ref[...]

    return call(
        kernel,
        (size // TILE,),
        [(d_output, columns(d_output.shape, offset))],
        [(out(tokens, size), columns((tokens, size)))],
    )[0]


def join(d_output, offset, pieces):
    tokens, size = d_output.shape[0], pieces[0][0].shape[1]

    def spec(at):
        return pl.BlockSpec((tokens, TILE), lambda i: (at, i))

    def kernel(*refs):
        for n, ref in enumerate(refs[:-1]):
            refs[-1][n * tokens : (n + 1) * tokens, :] = ref[...]

    shape = (tokens * (1 + len(pieces)), size)
    return call(
        kernel,
        (size // TILE,),
        [(d_output, columns(d_output.shape, offset))] + [(b, spec(at)) for b, at in pieces],
        [(out(*shape), columns(shape))],
    )[0]


def pack(rows, far, pick, held, parity):
    line, size = rows.shape
    count = pick.shape[1]
    per = count // held
    shape = (held, 2 * per, size)
    near, there = 1 + parity, 2 - parity

    places = [(group, start) for group in (there, 0) for start in (0, near)]

    def kernel(rows_ref, far_ref, *refs):
        picks, (here_ref, there_ref) = refs[:4], refs[4:]
        for k, pick_ref in enumerate(picks):
            chosen = mm(pick_ref[0], (rows_ref, far_ref)[k % 2][...]).astype(BF16)
            target, n = (there_ref, here_ref)[k // 2], k % 2
            for e in range(held):
                target[e, n * per : (n + 1) * per, :] = chosen[e * per : (e + 1) * per]

    def piece(place):
        at = PIECES.index(place)
        return pl.BlockSpec((1, count, line), lambda i: (at, 0, 0))

    return call(
        kernel,
        (size // TILE,),
        [(rows, columns(rows.shape)), (far, columns(far.shape))]
        + [(pick, piece(place)) for place in places],
        [(out(*shape), columns(shape)), (out(*shape), columns(shape))],
    )


def collect(here, came, turned, parity):
    held, half, size = here.shape
    block, total = turned.shape[2:]
    per = half // 2
    places = ((0, 1), (2, 3)) if parity == 0 else ((0, 2), (1, 3))

    def kernel(here_ref, came_ref, turned_ref, slots_ref, other_ref):
        for e in range(held):
            for ref, lines in zip((here_ref, came_ref), places):
                for n, at in enumerate(lines):
                    slots_ref[e, at * per : (at + 1) * per, :] = ref[e, n * per : (n + 1) * per]
            left = turned_ref[:, e].reshape(4 * block, total)
            product = mm(left, slots_ref[e])
            for n in range(4):
                other_ref[n, e] = product[n * block : (n + 1) * block].astype(BF16)

    return call(
        kernel,
        (size // TILE,),
        [
            (here, columns(here.shape)),
            (came, columns(came.shape)),
            (turned, pl.BlockSpec((4, held, block, total), lambda i: (1, 0, 0, 0))),
        ],
        [
            (out(held, total, size), columns((held, total, size))),
            (out(4, held, block, size), columns((4, held, block, size))),
        ],
    )


def own_product(slots, turned):
    held, total, size = slots.shape
    block = turned.shape[2]

    def kernel(slots_ref, turned_ref, mine_ref):
        for e in range(held):
            product = mm(turned_ref[:, e].reshape(4 * block, total), slots_ref[e])
            for n in range(4):
                mine_ref[n, e] = product[n * block : (n + 1) * block].astype(BF16)

    return call(
        kernel,
        (size // TILE,),
        [
            (slots, columns(slots.shape)),
            (turned, pl.BlockSpec((4, held, block, total), lambda i: (0, 0, 0, 0))),
        ],
        [(out(4, held, block, size), columns((4, held, block, size)))],
    )[0]


def add_parts(terms):
    shape = (len(terms),) + terms[0][0][0].shape[1:]
    flat = [term for group in terms for term in group]
    width = len(terms[0])

    def spec(at):
        return pl.BlockSpec((1,) + shape[1:-1] + (TILE,), lambda i: (at, 0, 0, i))

    def kernel(*refs):
        for n in range(len(terms)):
            value = 0.0
            for ref in refs[n * width : (n + 1) * width]:
                value = value + ref[0].astype(F32)
            refs[-1][n] = value.astype(BF16)

    return call(
        kernel,
        (shape[-1] // TILE,),
        [(array, spec(at)) for array, at in flat],
        [(out(*shape), columns(shape))],
    )[0]


def finish(parts, width):
    _, held, block, _ = parts[0][0].shape
    counts = [group[0].shape[3] // DEEP for group in parts]
    starts = [sum(counts[:n]) for n in range(len(counts))]
    terms = len(parts[0])

    def kernel(*refs):
        step = pl.program_id(0)
        for n, (start, count) in enumerate(zip(starts, counts)):

            @pl.when((step >= start) & (step < start + count))
            def _(n=n):
                value = 0.0
                for ref in refs[n * terms : (n + 1) * terms]:
                    value = value + ref[0].astype(F32)
                refs[-1][...] = value.astype(BF16)

    def spec(start, count):
        return pl.BlockSpec(
            (1, held, block, DEEP),
            lambda i: (0, 0, 0, jnp.minimum(jnp.maximum(i - start, 0), count - 1)),
        )

    shape = (held, block, width)
    return call(
        kernel,
        (width // DEEP,),
        [(part, spec(a, c)) for group, a, c in zip(parts, starts, counts) for part in group],
        [(out(*shape), pl.BlockSpec((held, block, DEEP), lambda i: (0, 0, i)))],
    )[0]


def chunk_specs(halves, offset, ff):
    rows = halves[0].shape[1]
    counts = [h.shape[2] // DEEP for h in halves]
    starts = [sum(counts[:n]) for n in range(len(halves))]

    def spec(start, count):
        return pl.BlockSpec(
            (1, rows, DEEP), lambda e, i: (e, 0, jnp.minimum(jnp.maximum(i - start, 0), count - 1))
        )

    specs = [spec(a, b) for a, b in zip(starts, counts)]
    return counts, starts, specs, pl.BlockSpec((1, ff, DEEP), lambda e, i: (e, 0, i + offset // DEEP))


def add_chunks(refs, starts, counts, lines, w_ref, sum_ref):
    step = pl.program_id(1)
    for n, (ref, start, count) in enumerate(zip(refs, starts, counts)):

        @pl.when((step >= start) & (step < start + count))
        def _(n=n, ref=ref):
            product = mm_turned(ref[0], w_ref[0])
            per = product.shape[0] // 2
            for k, line in enumerate(lines[n % 2]):
                sum_ref[line * per : (line + 1) * per, :] += product[k * per : (k + 1) * per]


HERE = ((0, 1), (0, 2))
CAME = ((2, 3), (1, 3))


def hidden_sums(halves, offset, w_down):
    held, rows, _ = halves[0].shape
    ff, total = w_down.shape[1], 2 * rows
    counts, starts, specs, w_spec = chunk_specs(halves, offset, ff)

    def kernel(*refs):
        w_ref, sum_ref, acc_ref = refs[len(halves) :]

        @pl.when(pl.program_id(1) == 0)
        def _():
            acc_ref[...] = jnp.zeros_like(acc_ref)

        add_chunks(refs, starts, counts, HERE, w_ref, acc_ref)

        @pl.when(pl.program_id(1) == sum(counts) - 1)
        def _():
            sum_ref[0] = acc_ref[...]

    return call(
        kernel,
        (held, sum(counts)),
        list(zip(halves, specs)) + [(w_down, w_spec)],
        [(out(held, total, ff, dtype=F32), pl.BlockSpec((1, total, ff), lambda e, i: (e, 0, 0)))],
        scratch=[pltpu.VMEM((total, ff), F32)],
    )[0]


def hidden_end(at, key, gate, hidden, sums, halves, w_down):
    held, sources, cap, ff = hidden.shape
    total = sums[0].shape[1]
    tokens = key.shape[1]
    counts, starts, specs, w_spec = chunk_specs(halves, 0, ff)

    def kernel(at_ref, key_ref, gate_ref, hidden_ref, *refs):
        sums_refs, refs = refs[: len(sums)], refs[len(sums) :]
        w_ref, d_hidden_ref, grad_ref, acc_ref = refs[len(halves) :]

        @pl.when(pl.program_id(1) == 0)
        def _():
            acc_ref[...] = sum(ref[0] for ref in sums_refs)

        add_chunks(refs, starts, counts, CAME, w_ref, acc_ref)

        def end(e):
            for r in range(sources):
                row = r * held + e
                hits = slot_hits(key_ref, row, cap)
                weight = jnp.sum(
                    jnp.where(hits, gate_ref[row : row + 1, :], 0.0), axis=1, keepdims=True
                )
                value = acc_ref[r * cap : (r + 1) * cap, :]
                place = at_ref[r]
                d_hidden_ref[0, place] = (value * weight).astype(BF16)
                dots = jnp.sum(value * hidden_ref[0, place].astype(F32), axis=1, keepdims=True)
                grad_ref[place, e : e + 1, :] = jnp.sum(
                    jnp.where(hits, dots, 0.0), axis=0, keepdims=True
                )

        for e in range(held):

            @pl.when((pl.program_id(1) == sum(counts) - 1) & (pl.program_id(0) == e))
            def _(e=e):
                end(e)

    by_expert = pl.BlockSpec((1, sources, cap, ff), lambda e, i: (e, 0, 0, 0))
    return call(
        kernel,
        (held, sum(counts)),
        [
            (at, SMEM),
            (key, whole(key.shape)),
            (gate, whole(gate.shape)),
            (hidden, by_expert),
        ]
        + [(part, pl.BlockSpec((1, total, ff), lambda e, i: (e, 0, 0))) for part in sums]
        + list(zip(halves, specs))
        + [(w_down, w_spec)],
        [
            (out(*hidden.shape), by_expert),
            (out(sources, held, tokens, dtype=F32), whole((sources, held, tokens))),
        ],
        scratch=[pltpu.VMEM((total, ff), F32)],
    )


def shards(d_output, gate_values, routes, hidden_saved, w_down):
    ORDER.token = None
    tokens, width = d_output.shape
    hidden = hidden_saved[0]
    held, sources, cap, ff = hidden.shape

    section, group = lax.axis_index("section"), lax.axis_index("expert")
    z, core, y, x = section // 2, section % 2, group // 4, group % 4
    masks = jnp.stack([0 * core, 1 + 2 * core, 3 - 2 * core, 0 * core + 2])
    first_at = jnp.where(core == 0, x, y) ^ masks
    second_at = jnp.where(core == 0, y, x) ^ masks
    up_first, up_second = jnp.where(core == 0, 1, 4), jnp.where(core == 0, 4, 1)
    source_at = (second_at[:, None] * up_second + first_at[None, :] * up_first).reshape(-1)
    group_at = second_at[:4] * up_second + first_at[0] * up_first
    experts = (group_at[:, None] * held + jnp.arange(held)[None, :]).reshape(-1)
    section_at = jnp.arange(8)
    met = (section_at // 2) ^ z
    place = jnp.where(met == 2, 3, jnp.where(met == 0, 0, jnp.where((met == 1) == (section_at % 2 == 0), 2, 1)))
    is_mine = section_at % 2 == core
    at = jnp.concatenate([source_at, experts, jnp.where(is_mine, place, 4 + place)]).astype(jnp.int32)

    offsets = [sum(CHUNKS[:n]) for n in range(len(CHUNKS))]
    info = jnp.concatenate([routes.astype(F32), gate_values.astype(F32)], axis=1).T
    count = len(CHUNKS)
    one, two, rows, far, here, came, slots = ([None] * count for _ in range(7))
    hidden_parts = [None] * (count // 2)
    got, mine, passed, more = ([None] * count for _ in range(4))
    for n in range(2):
        own = d_output[:, offsets[n] : offsets[n] + CHUNKS[n]]
        one[n] = send(own, along("first", 0, n % 2))

    for step in PLAN:
        kind, n = step[0], int(step[1:2].strip("-") or 0)
        parity = n % 2
        ORDER.room = END_LIMIT if kind == "H" else VMEM_LIMIT
        ORDER.cost = 0 if step.endswith("-") else 20
        if kind == "o":
            one[n] = send(own_rows(d_output, offsets[n], CHUNKS[n]), along("first", 0, parity))
        elif kind == "I":
            all_info = lax.all_to_all(share(info, sources), "expert", 0, 0, tiled=True)
        elif kind == "P":
            pick, key, gate = prepare(at, all_info, cap, held)
        elif kind == "T":
            turned = turn_hidden(at, key, gate, hidden)
        elif kind == "a":
            two[n] = send(join(d_output, offsets[n], [(one[n], 0)]), along("first", 1, parity))
        elif kind == "r":
            came_rows = [(one[n], 0), (two[n], 0), (two[n], 1)]
            if parity == 1:
                came_rows = [(two[n], 0), (one[n], 0), (two[n], 1)]
            rows[n] = join(d_output, offsets[n], came_rows)
            far[n] = send(rows[n], along("second", 0, parity))
        elif kind == "p":
            here[n], there = pack(rows[n], far[n], pick, held, parity)
            came[n] = send(there, along("second", 1, parity))
        elif kind == "w":
            slots[n], other = collect(here[n], came[n], turned, parity)
            got[n] = send(other, SWAP)
        elif kind == "m":
            mine[n] = own_product(slots[n], turned)
        elif kind == "s":
            sums = add_parts([[(mine[n], k), (got[n], k)] for k in (2 - parity, 3)])
            passed[n] = send(sums, along("z", 0, parity))
        elif kind == "t":
            sums = add_parts([[(mine[n], 1 + parity), (got[n], 1 + parity), (passed[n], 1)]])
            more[n] = send(sums, along("z", 1, parity))
        elif kind == "e":
            parts = [(mine[k], got[k], passed[k], more[k]) for k in range(count)]
            d_weight = finish(parts, width)
        elif kind == "h":
            hidden_parts[n] = hidden_sums(here[2 * n : 2 * n + 2], offsets[2 * n], w_down)
        elif kind == "H":
            d_hidden, token_grad = hidden_end(at, key, gate, hidden, hidden_parts, came, w_down)
    returned = lax.all_to_all(token_grad, "expert", 0, 0, tiled=True).reshape(-1, tokens)
    chosen = routes.T[None] == jnp.arange(sources * held)[:, None, None]
    d_gate = jnp.sum(jnp.where(chosen, returned[:, None, :], 0.0), axis=0).T
    return (d_hidden[None], d_weight, d_gate)


def solution(mesh):
    placed = (
        P(("section", "expert"), None),
        P(("section", "expert"), None),
        P(("section", "expert"), None),
        P("section", "expert", None, None, None),
        P("expert", None, None),
    )
    return jax.shard_map(
        shards,
        mesh=mesh,
        in_specs=placed,
        out_specs=(
            P("section", "expert", None, None, None),
            P("expert", "section", None),
            P(("section", "expert"), None),
        ),
        check_vma=False,
    )
```
